256 devices in a mesh: vocab: 64 (over x, z, core), rows: 4 (over y).
Axes of the slice: x: 4, y: 4, z: 8, core: 2. Of those that a mesh axis runs over, the one named last changes fastest.
Arguments:
- hidden: bfloat16 [1024, 4608], P('rows'), may hold values from -6 to 6
- norm_gain: bfloat16 [4608], replicated, may hold values from 0.5 to 1.5
- embed_table: bfloat16 [131072, 4608], P('vocab', 'rows'), may hold values from -1 to 1
- tokens: int32 [1024], P('rows'), may hold values from 0 to 131071
- parents: int32 [1024], P('rows'), may hold values from 0 to 7
- prev_scores: float32 [1024], P('rows'), may hold values from -30 to -1
- lengths: int32 [1024], P('rows'), may hold values from 1 to 128
Outputs:
- log_probs: float32 [1024, 131072], P('rows', 'vocab')
- chosen_lp: float32 [1024], P('rows')
- normalized: float32 [1024], P('rows')
- next_embed: bfloat16 [1024, 4608], P('rows')
The draws below stay inside these ranges and needn't reach their ends.
All inputs are finite; a program needn't handle non-finite values.
Results may differ from the reference program's by a relative error of at most 0.0045.
Values may be sent and summed in bfloat16 or wider, within the bound.
No kernel may reach another device: no remote copies, remote signals or barrier semaphores. Data moves between devices by JAX's collectives and lax.ppermute only.
A program may use at most 128 MiB of HBM per device.

```python
import math
import jax
import jax.numpy as jnp
from jax import lax

D = 4608
BEAMS = 8
ROWS = 1024
VOCAB = 131072


def draw_embed_table(key, part):
    key = jax.random.fold_in(key, 11)
    key_entries, key_scales = jax.random.split(key, 2)
    ramp = 0.85 + 0.3 * jnp.arange(VOCAB, dtype=jnp.float32) / VOCAB
    row_scale = jnp.exp(jax.random.uniform(key_scales, (VOCAB,), jnp.float32, math.log(0.5), math.log(2.5)))
    entries = jnp.clip(jax.random.normal(key_entries, (VOCAB, D), jnp.float32), -6.0, 6.0)
    factor = ramp * row_scale * (3.0 / math.sqrt(D))
    return jnp.clip(entries * factor[:, None], -1.0, 1.0).astype(jnp.bfloat16)


def touch_ends(result, key, low, top_value):
    longest = result.shape.index(max(result.shape))
    spots = []
    for shift in (0, 1):
        where = [jax.random.randint(jax.random.fold_in(key, axis), (), 0, length) for axis, length in enumerate(result.shape)]
        where[longest] = (where[longest] + shift) % result.shape[longest]
        spots.append(tuple(where))
    return result.at[spots[0]].set(low).at[spots[1]].set(top_value)


def shard_levels(own_key, extent, cuts, smallest, high):
    factor_of, own = 1.0, jax.random.fold_in(own_key, 6)
    for dim, shards_of in cuts:
        draws = jnp.exp(jax.random.uniform(jax.random.fold_in(own, dim), (shards_of,), jnp.float32, smallest / len(cuts), high / len(cuts)))
        factor_of = factor_of * jnp.repeat(draws, extent[dim] // shards_of).reshape([-1 if axis == dim else 1 for axis in range(len(extent))])
    return factor_of


def bell_draw(own_key, dims, deviation, most, cuts=(), kind=jnp.bfloat16):
    loudness = shard_levels(own_key, dims, cuts, -0.22, 0.18) if cuts else 1.0
    result = jax.random.normal(own_key, dims, jnp.float32) * deviation * loudness
    return jnp.minimum(jnp.maximum(result, -most), most).astype(kind)


def setup_inputs(seed: int = 0) -> dict:
    arg_keys = jax.random.split(jax.random.key(seed), 8)
    return {
        "hidden": bell_draw(arg_keys[0], (ROWS, D), 1.0, 6.0, ((0, 4),)),
        "norm_gain": jnp.clip(1.0 + 0.1 * jax.random.normal(arg_keys[1], (D,), jnp.float32), 0.5, 1.5).astype(jnp.bfloat16),
        "embed_table": draw_embed_table(jax.random.fold_in(arg_keys[7], 71), 0),
        "tokens": touch_ends(jax.random.randint(arg_keys[3], (ROWS,), 0, VOCAB), jax.random.fold_in(arg_keys[3], 1), 0, VOCAB - 1).astype(jnp.int32),
        "parents": touch_ends(jax.random.randint(arg_keys[4], (ROWS,), 0, BEAMS), jax.random.fold_in(arg_keys[4], 1), 0, BEAMS - 1).astype(jnp.int32),
        "prev_scores": jnp.clip(-30.0 + 29.0 * jax.random.uniform(arg_keys[5], (ROWS,), jnp.float32) ** shard_levels(arg_keys[5], (ROWS,), ((0, 4),), -0.2, 0.2), -30.0, -1.0),
        "lengths": touch_ends(jax.random.randint(arg_keys[6], (ROWS,), 1, 129), jax.random.fold_in(arg_keys[6], 1), 1, 128).astype(jnp.int32),
    }


soft_cap = 30.0
length_power = 0.6
norm_eps = 1e-06

def reference(hidden, norm_gain, embed_table, tokens, parents, prev_scores, lengths):
    states = hidden.astype(jnp.float32)
    meansq = lax.optimization_barrier(jnp.mean(states * states, axis=-1, keepdims=True))
    normed = (states * lax.rsqrt(meansq + norm_eps) * norm_gain.astype(jnp.float32)).astype(jnp.bfloat16)
    logits = lax.dot_general(normed, embed_table, (((1,), (1,)), ((), ())), preferred_element_type=jnp.float32)
    capped = soft_cap * jnp.tanh(logits / soft_cap)
    lse = jnp.log(lax.optimization_barrier(jnp.sum(jnp.exp(capped), axis=1)))
    log_probs = capped - lse[:, None]
    parent_rows = jnp.arange(ROWS, dtype=jnp.int32) // BEAMS * BEAMS + parents
    chosen_lp = capped[parent_rows, tokens] - lse[parent_rows]
    penalty = jnp.power((5.0 + lengths.astype(jnp.float32)) / 6.0, length_power)
    normalized = (prev_scores[parent_rows] + chosen_lp) / penalty
    next_embed = (embed_table[tokens].astype(jnp.float32) * math.sqrt(D)).astype(jnp.bfloat16)
    return (log_probs, chosen_lp, normalized, next_embed)
```

```python
import math

import jax
import jax.numpy as jnp
from jax import lax
from jax.sharding import Mesh, PartitionSpec as P

BEAMS = 8

soft_cap = 30.0
length_power = 0.6
norm_eps = 1e-06

VOC = ("x", "z", "c")
NX, NZ, NC, NY = 4, 8, 2, 4


def shift(value, axis, size, step):
    return lax.ppermute(value, axis, [(i, (i + step) % size) for i in range(size)])


def exchange(value, axes):
    return lax.all_to_all(value, axes, 0, 0, tiled=True)


def dot_nt(left, right):
    return lax.dot_general(left, right, (((1,), (1,)), ((), ())), preferred_element_type=jnp.float32)


def lookup(tokens, embed_table, scale):
    voc_rows, depth = embed_table.shape
    shard = lax.axis_index(VOC)
    core = lax.axis_index("c")
    rows = tokens.shape[0]
    part = rows // (NC * NX)
    halves = tokens.reshape(NC, NX, 1, part)
    ordered = jnp.where(core == 0, halves, halves[::-1])
    both = jnp.concatenate(
        [ordered] + [shift(ordered, "y", NY, step) for step in (1, 2, 3)], axis=2
    )
    y = lax.axis_index("y")
    order = (y - jnp.arange(NY)) % NY
    planes = sum(
        jnp.where((order == j)[None, None, :, None], both[:, :, j : j + 1], 0) for j in range(NY)
    )
    local_col = (planes - shard * voc_rows).reshape(NC, rows * NY // NC)

    def rows_of(col):
        hot = (col[:, None] == jnp.arange(voc_rows, dtype=jnp.int32)[None, :]).astype(jnp.bfloat16)
        found = jnp.dot(hot, embed_table, preferred_element_type=jnp.float32)
        return (found * scale).astype(jnp.bfloat16)

    other = shift(rows_of(local_col[1]), "c", NC, 1)
    mine = (rows_of(local_col[0]) + other).reshape(NX, NY * part, depth)
    mine = jnp.sum(exchange(mine, "x"), axis=0)
    mine = exchange(mine.reshape(NY, part, depth), "y")
    mine = jnp.sum(exchange(mine.reshape(NZ, NY * part // NZ, depth), "z"), axis=0)
    mine = exchange(jnp.broadcast_to(mine[None], (NZ,) + mine.shape), "z")
    mine = lax.all_gather(mine.reshape(NY, part, depth), "x")
    other = shift(mine, "c", NC, 1)
    full = jnp.stack([jnp.where(core == 0, mine, other), jnp.where(core == 0, other, mine)])
    return full.transpose(0, 1, 3, 2, 4).reshape(rows, NY * depth)


def local(hidden, norm_gain, embed_table, tokens, parents, prev_scores, lengths):
    shard = lax.axis_index(VOC)
    core = lax.axis_index("c")
    y = lax.axis_index("y")
    voc_rows, depth = embed_table.shape
    row_count, width = hidden.shape
    half = row_count // NC
    half_voc = voc_rows // 2
    scale = math.sqrt(width)

    gain_part = lax.dynamic_slice(norm_gain, (y * depth,), (depth,)).astype(jnp.float32)

    def gained(features):
        return (features.astype(jnp.float32) * gain_part).astype(jnp.bfloat16)

    def fetch(step):
        there = (y + step) % NY
        piece = lax.dynamic_slice(hidden, (core * half, there * depth), (half, depth))
        mine = shift(piece, "y", NY, step)
        other = shift(mine, "c", NC, 1)
        return gained(
            jnp.concatenate(
                [jnp.where(core == 0, mine, other), jnp.where(core == 0, other, mine)], axis=0
            )
        )

    upper, lower = embed_table[:half_voc], embed_table[half_voc:]
    far = fetch(2)
    far_a = shift(dot_nt(far, upper).astype(jnp.bfloat16), "y", NY, 1)
    far_b = shift(dot_nt(far, lower).astype(jnp.bfloat16), "y", NY, 3)
    ahead = fetch(3)
    behind = fetch(1)
    left_b = shift(dot_nt(ahead, lower).astype(jnp.bfloat16), "y", NY, 1)
    right_a = shift(dot_nt(behind, upper).astype(jnp.bfloat16), "y", NY, 3)
    left_a = shift((dot_nt(ahead, upper) + far_a.astype(jnp.float32)).astype(jnp.bfloat16), "y", NY, 1)
    right_b = shift((dot_nt(behind, lower) + far_b.astype(jnp.float32)).astype(jnp.bfloat16), "y", NY, 3)
    own = gained(lax.dynamic_slice(hidden, (0, y * depth), (row_count, depth)))
    states = hidden.astype(jnp.float32)
    meansq = jnp.mean(states * states, axis=-1, keepdims=True)
    row_scale = lax.rsqrt(meansq + norm_eps)

    def total(part, table_part, one, two):
        return dot_nt(part, table_part) + one.astype(jnp.float32) + two.astype(jnp.float32)

    logits = row_scale * jnp.concatenate(
        [total(own, upper, left_a, right_a), total(own, lower, left_b, right_b)], axis=1
    )

    local_col = tokens - shard * voc_rows
    inside = (local_col >= 0) & (local_col < voc_rows)
    clipped_col = jnp.clip(local_col, 0, voc_rows - 1)
    capped = soft_cap * jnp.tanh(logits / soft_cap)
    sum_exp = jnp.sum(jnp.exp(capped), axis=1)
    parent_rows = jnp.arange(row_count, dtype=jnp.int32) // BEAMS * BEAMS + parents
    chosen_local = jnp.where(inside, capped[parent_rows, clipped_col], 0.0)
    sums = jnp.concatenate([sum_exp, chosen_local])[None]
    sums = jnp.sum(exchange(jnp.broadcast_to(sums, (NX * NZ * NC, 2 * row_count)), VOC), axis=0)
    lse = jnp.log(sums[:row_count])
    log_probs = capped - lse[:, None]
    chosen_lp = sums[row_count:] - lse[parent_rows]
    penalty = jnp.power((5.0 + lengths.astype(jnp.float32)) / 6.0, length_power)
    normalized = (prev_scores[parent_rows] + chosen_lp) / penalty
    next_embed = lookup(tokens, embed_table, scale)
    return (log_probs, chosen_lp, normalized, next_embed)


def solution(mesh):
    split = Mesh(mesh.devices.reshape(NX, NZ, NC, NY), VOC + ("y",))
    placed = (P("y", None), P(), P(VOC, "y"), P("y"), P("y"), P("y"), P("y"))
    return jax.shard_map(
        local,
        mesh=split,
        in_specs=placed,
        out_specs=(P("y", VOC), P("y"), P("y"), P("y", None)),
        check_vma=False,
    )
```

```python
import math

import jax
import jax.numpy as jnp
from jax import lax
from jax.experimental import pallas as pl
from jax.experimental.pallas import tpu as pltpu
from jax.sharding import Mesh, PartitionSpec as P

BEAMS = 8

soft_cap = 30.0
length_power = 0.6
norm_eps = 1e-06

VOC = ("x", "z", "c")
NX, NZ, NC, NY = 4, 8, 2, 4
BLOCK = 256
CHUNK = 512
LANES = 128
VMEM = 36 * 1024 * 1024


def shift(value, axis, size, step):
    return lax.ppermute(value, axis, [(i, (i + step) % size) for i in range(size)])


def exchange(value, axes):
    return lax.all_to_all(value, axes, 0, 0, tiled=True)


def dot_nt(left, right):
    return lax.dot_general(left, right, (((1,), (1,)), ((), ())), preferred_element_type=jnp.float32)


def call(body, outs, args, after=(), smem=0, far_args=0, scratch=()):
    def whole(*refs):
        count = len(args) + len(after)
        tick = refs[count + len(outs)]
        tick[...] = jnp.zeros(tick.shape, tick.dtype)
        body(*refs[: len(args)], *refs[count : count + len(outs)], *refs[count + len(outs) + 1 :])

    spaces = [pltpu.SMEM] * smem + [pltpu.HBM] * far_args
    spaces += [pltpu.VMEM] * (len(args) - len(spaces)) + [pl.ANY] * len(after)
    args = [
        pltpu.with_memory_space_constraint(arg, pltpu.HBM) if space is pltpu.HBM else arg
        for arg, space in zip(args, spaces)
    ]
    out_specs = []
    for out in outs:
        inside = isinstance(out, jax.ShapeDtypeStruct)
        out_specs.append(pl.BlockSpec(memory_space=pltpu.VMEM if inside else pltpu.HBM))
    return pl.pallas_call(
        whole,
        out_shape=list(outs) + [jax.ShapeDtypeStruct((8, LANES), jnp.float32)],
        in_specs=[pl.BlockSpec(memory_space=space) for space in spaces],
        out_specs=out_specs + [pl.BlockSpec(memory_space=pltpu.VMEM)],
        scratch_shapes=list(scratch),
        cost_estimate=pl.CostEstimate(flops=0, bytes_accessed=0, transcendentals=0),
        compiler_params=pltpu.CompilerParams(vmem_limit_bytes=VMEM),
    )(*args, *after)


def like(shape, dtype=jnp.bfloat16):
    return jax.ShapeDtypeStruct(shape, dtype)


def start_all(copies):
    for copy in copies:
        copy.start()
    return copies


def piece_of(hidden_ref, half, quarter):
    rows, width = hidden_ref.shape
    count, depth = rows // NC, width // NY
    return hidden_ref.at[
        pl.ds(pl.multiple_of(half * count, count), count),
        pl.ds(pl.multiple_of(quarter * depth, LANES), depth),
    ]


def gained(features, gain_ref, quarter):
    depth = features.shape[1]
    gain = gain_ref[:, pl.ds(pl.multiple_of(quarter * depth, LANES), depth)]
    return (features.astype(jnp.float32) * gain.astype(jnp.float32)).astype(features.dtype)


def cut_pieces(place, hidden, gain, after):
    rows, width = hidden.shape
    shape = (NY, rows // NC, width // NY)

    def body(place_ref, hidden_ref, gain_ref, out, held, sems):
        copies = start_all(
            [
                pltpu.make_async_copy(piece_of(hidden_ref, place_ref[0], n), held.at[n], sems.at[n])
                for n in range(NY)
            ]
        )
        for n in range(NY):
            copies[n].wait()
            out[n] = gained(held[n], gain_ref, n)

    return call(
        body, [like(shape)], [place, hidden, gain], after, smem=1, far_args=1,
        scratch=[pltpu.VMEM(shape, hidden.dtype), pltpu.SemaphoreType.DMA((NY,))],
    )


def pick_rows(cols, table, scale, after):
    voc_rows, depth = table.shape
    steps = voc_rows // CHUNK
    count = cols.shape[0] // NC
    blocks = 1
    block = count // blocks

    def body(table_ref, col_ref, sent, kept, held, found, sems):
        load = start_all(
            [
                pltpu.make_async_copy(
                    table_ref.at[n * CHUNK : (n + 1) * CHUNK], held.at[n * CHUNK : (n + 1) * CHUNK], sems.at[n]
                )
                for n in range(steps)
            ]
        )
        put = []
        for n in range(NC * blocks):
            ids = lax.broadcasted_iota(jnp.int32, (block, voc_rows), 1)
            at = (n + blocks) % (NC * blocks) * block
            hot = jnp.where(ids == col_ref[at : at + block], 1.0, 0.0).astype(held.dtype)
            if n == 0:
                for copy in load:
                    copy.wait()
            picked = jnp.dot(hot, held[...], preferred_element_type=jnp.float32)
            found[n] = (picked * scale).astype(found.dtype)
            out = (sent, kept)[n // blocks].at[n % blocks * block : (n % blocks + 1) * block]
            put.append(pltpu.make_async_copy(found.at[n], out, sems.at[steps + n]))
            put[-1].start()
        for copy in put:
            copy.wait()

    return call(
        body, [pltpu.HBM((count, depth), table.dtype)] * 2, [table, cols], after, far_args=1,
        scratch=[
            pltpu.VMEM((voc_rows, depth), table.dtype),
            pltpu.VMEM((NC * blocks, block, depth), table.dtype),
            pltpu.SemaphoreType.DMA((steps + NC * blocks,)),
        ],
    )


def products(place, mine, other, table, after):
    half, depth = mine.shape[1:]
    voc_rows = table.shape[0]
    steps = voc_rows // CHUNK
    rows = NC * half
    distances = (2, 1, 3, 0)

    def body(place_ref, mine_ref, other_ref, table_ref, *refs):
        outs = refs[: NY + 1]
        feats, held, results, sems = refs[NY + 1 :]
        get = []
        for n, distance in enumerate(distances):
            plane = lax.rem(place_ref[1] + distance, NY)
            for k, ref in enumerate((mine_ref, other_ref)):
                start = n * rows + k * half
                get.append(
                    pltpu.make_async_copy(ref.at[plane], feats.at[start : start + half], sems.at[0, NC * n + k])
                )
        load = [
            pltpu.make_async_copy(table_ref.at[n * CHUNK : (n + 1) * CHUNK], held.at[n], sems.at[1, n])
            for n in range(steps)
        ]
        start_all(get + load)
        put = []
        for step in range(steps):
            load[step].wait()
            if step == 0:
                for copy in get:
                    copy.wait()
            found = jnp.dot(feats[...], held[step].T, preferred_element_type=jnp.float32)
            results[step] = found.astype(results.dtype)
            for n in range(NY):
                if n == 0:
                    at = step % (steps // 2) * CHUNK
                    out = outs[step // (steps // 2)].at[:, at : at + CHUNK]
                else:
                    out = outs[n + 1].at[:, step * CHUNK : (step + 1) * CHUNK]
                piece = results.at[step, n * rows : (n + 1) * rows]
                put.append(pltpu.make_async_copy(piece, out, sems.at[2 + n, step]))
                put[-1].start()
        for copy in put:
            copy.wait()

    kind = table.dtype
    return call(
        body,
        [pltpu.HBM((rows, voc_rows // 2), kind)] * 2 + [pltpu.HBM((rows, voc_rows), kind)] * 3,
        [place, mine, other, table], after, smem=1, far_args=3,
        scratch=[
            pltpu.VMEM((NY * rows, depth), kind),
            pltpu.VMEM((steps, CHUNK, depth), kind),
            pltpu.VMEM((steps, NY * rows, CHUNK), kind),
            pltpu.SemaphoreType.DMA((2 + NY, 2 * NY)),
        ],
    )


def add_halves(ahead, behind, far_a, far_b, after):
    rows, voc_rows = ahead.shape
    wide = voc_rows // 2
    part = rows // NC

    def body(ahead_ref, behind_ref, a_ref, b_ref, left, right, held, sems):
        sides = ((ahead_ref, a_ref, left, 0), (behind_ref, b_ref, right, wide))
        load, put = [], []
        for n, (near, far, out, start) in enumerate(sides):
            for k in range(NC):
                at = slice(k * part, (k + 1) * part)
                load.append(
                    [
                        pltpu.make_async_copy(near.at[at], held.at[n, at], sems.at[n, k]),
                        pltpu.make_async_copy(far.at[at], held.at[2, at, start : start + wide], sems.at[2 + n, k]),
                    ]
                )
                put.append(pltpu.make_async_copy(held.at[n, at], out.at[at], sems.at[4 + n, k]))
        for pair in load:
            start_all(pair)
        for m, pair in enumerate(load):
            n, k = divmod(m, NC)
            for copy in pair:
                copy.wait()
            at, cols = slice(k * part, (k + 1) * part), slice(n * wide, (n + 1) * wide)
            total = held[n, at, cols].astype(jnp.float32) + held[2, at, cols].astype(jnp.float32)
            held[n, at, cols] = total.astype(held.dtype)
            put[m].start()
        for copy in put:
            copy.wait()

    return call(
        body, [pltpu.HBM(ahead.shape, ahead.dtype)] * 2, [ahead, behind, far_a, far_b], after, far_args=4,
        scratch=[pltpu.VMEM((3, rows, voc_rows), ahead.dtype), pltpu.SemaphoreType.DMA((6, NC))],
    )


def cap_and_sum(place, own, left, right, row_scale, cols, parents, after):
    rows, voc_rows = own.shape
    half = rows // NC
    peers = NX * NZ * NC
    wide = voc_rows // 2

    def body(
        place_ref, own_ref, left_ref, right_ref, scale_ref, col_ref, par_ref, capped_ref, stats_ref,
        held, sems,
    ):
        load = [
            [
                [
                    pltpu.make_async_copy(
                        ref.at[turn * half : (turn + 1) * half, side * wide : (side + 1) * wide],
                        held.at[turn, side, n],
                        sems.at[turn, side, n],
                    )
                    for n, ref in enumerate((own_ref, left_ref, right_ref))
                ]
                for side in range(2)
            ]
            for turn in range(NC)
        ]
        for turn in range(NC):
            for side in range(2):
                start_all(load[turn][side])
        lane = lax.broadcasted_iota(jnp.int32, (half, LANES), 1)
        for turn in range(NC):
            natural = place_ref[0] if turn == 0 else 1 - place_ref[0]
            here = pl.ds(pl.multiple_of(natural * half, half), half)
            scale, col, pick = (
                jnp.broadcast_to(ref[:, here].astype(jnp.float32), (LANES, half)).T
                for ref in (scale_ref, col_ref, par_ref)
            )
            col, pick = col.astype(jnp.int32), pick.astype(jnp.int32)
            total = jnp.zeros((half, LANES), jnp.float32)
            chosen = jnp.zeros((half, LANES), jnp.float32)
            for start in range(0, voc_rows, LANES):
                side = start // wide
                if start % wide == 0:
                    for copy in load[turn][side]:
                        copy.wait()
                at = slice(start % wide, start % wide + LANES)
                logit = sum(held[turn, side, n, :, at].astype(jnp.float32) for n in range(3))
                capped = soft_cap * jnp.tanh(logit * scale / soft_cap)
                capped_ref[here, start : start + LANES] = capped
                total += jnp.exp(capped)
                moved = jnp.concatenate(
                    [
                        jnp.take_along_axis(capped[g : g + BEAMS], pick[g : g + BEAMS], axis=0)
                        for g in range(0, half, BEAMS)
                    ],
                    axis=0,
                )
                chosen += jnp.where(lane + start == col, moved, 0.0)
            for n, part in enumerate((total, chosen)):
                row = jnp.sum(part.T, axis=0, keepdims=True)
                at = pl.ds(pl.multiple_of(n * rows + natural * half, LANES), half)
                stats_ref[:, at] = jnp.broadcast_to(row, (peers, half))

    return call(
        body, [like((rows, voc_rows), jnp.float32), like((peers, 2 * rows), jnp.float32)],
        [place, own, left, right, row_scale, cols, parents], after, smem=1, far_args=3,
        scratch=[pltpu.VMEM((NC, 2, 3, half, wide), own.dtype), pltpu.SemaphoreType.DMA((NC, 2, 3))],
    )


def score(stats, parents, prev_scores, penalty, filler):
    rows = parents.shape[1]

    def body(stats_ref, par_ref, prev_ref, pen_ref, column, chosen_ref, norm_ref, fill):
        fill[...] = jnp.zeros(fill.shape, fill.dtype)
        sums = jnp.sum(stats_ref[...], axis=0, keepdims=True)
        lse = jnp.log(sums[:, :rows])
        sub = lax.broadcasted_iota(jnp.int32, (LANES, LANES), 0)
        lane = lax.broadcasted_iota(jnp.int32, (1, LANES), 1)
        for h in range(rows // LANES):
            at = slice(h * LANES, (h + 1) * LANES)

            def down(row):
                return jnp.broadcast_to(row, (LANES, LANES)).T

            lse_col = down(lse[:, at])
            column[at] = lse_col
            hit = sub == lane // BEAMS * BEAMS + par_ref[:, at]
            lse_par = jnp.sum(jnp.where(hit, lse_col, 0.0), axis=0, keepdims=True)
            prev_par = jnp.sum(jnp.where(hit, down(prev_ref[:, at]), 0.0), axis=0, keepdims=True)
            chosen = sums[:, rows + h * LANES : rows + (h + 1) * LANES] - lse_par
            chosen_ref[:, at] = chosen
            norm_ref[:, at] = (prev_par + chosen) / pen_ref[:, at]

    row = like((1, rows), jnp.float32)
    return call(
        body, [like((rows, LANES), jnp.float32), row, row, like(filler)],
        [stats, parents, prev_scores, penalty],
    )


def subtract(capped, column):
    rows, voc_rows = capped.shape
    steps = 4

    def body(capped_ref, column_ref, log_ref):
        for start in range(0, voc_rows, LANES):
            at = slice(start, start + LANES)
            log_ref[:, at] = capped_ref[:, at] - column_ref[...]

    block = pl.BlockSpec((rows // steps, voc_rows), lambda i: (i, 0))
    return pl.pallas_call(
        body,
        out_shape=like((rows, voc_rows), jnp.float32),
        grid=(steps,),
        in_specs=[block, pl.BlockSpec((rows // steps, LANES), lambda i: (i, 0))],
        out_specs=block,
        cost_estimate=pl.CostEstimate(flops=0, bytes_accessed=0, transcendentals=0),
        compiler_params=pltpu.CompilerParams(vmem_limit_bytes=VMEM),
    )(capped, column)


def add(one, two, after):
    count, depth = one.shape
    cuts = [slice(start, start + LANES) for start in range(0, count, LANES)]

    def body(one_ref, two_ref, out, held, total, sems):
        load = [
            [
                pltpu.make_async_copy(ref.at[at], held.at[k, at], sems.at[k, n])
                for k, ref in enumerate((one_ref, two_ref))
            ]
            for n, at in enumerate(cuts)
        ]
        put = [pltpu.make_async_copy(total.at[at], out.at[at], sems.at[2, n]) for n, at in enumerate(cuts)]
        for pair in load:
            start_all(pair)
        for n, at in enumerate(cuts):
            for copy in load[n]:
                copy.wait()
            total[at] = held[0, at] + held[1, at]
            put[n].start()
        for copy in put:
            copy.wait()

    return call(
        body, [pltpu.HBM(one.shape, one.dtype)], [one, two], after, far_args=2,
        scratch=[
            pltpu.VMEM((2, *one.shape), one.dtype),
            pltpu.VMEM(one.shape, one.dtype),
            pltpu.SemaphoreType.DMA((3, len(cuts))),
        ],
    )


def sum_rows(stacked, copies, after=()):
    terms, rows, depth = stacked.shape

    def body(in_ref, out):
        found = in_ref[0].astype(jnp.float32)
        for n in range(1, terms):
            found = found + in_ref[n].astype(jnp.float32)
        for n in range(copies):
            out[n] = found.astype(stacked.dtype)

    return call(body, [like((copies, rows, depth))], [stacked], after)


def assemble(place, mine, other, after):
    parts = len(mine)
    quarters, part, depth = mine[0].shape

    def body(place_ref, *refs):
        *pieces, out, sems = refs
        copies = []
        for n, ref in enumerate(pieces):
            core = place_ref[0] if n < parts else 1 - place_ref[0]
            x = lax.rem(place_ref[2] + parts - n % parts, parts)
            at = pl.ds(pl.multiple_of((core * parts + x) * part, part), part)
            for q in range(quarters):
                copies.append(
                    pltpu.make_async_copy(
                        ref.at[q], out.at[at, q * depth : (q + 1) * depth], sems.at[n, q]
                    )
                )
        start_all(copies)
        for copy in copies:
            copy.wait()

    return call(
        body, [pltpu.HBM((NC * parts * part, quarters * depth), mine[0].dtype)],
        [place, *mine, *other], after, smem=1,
        scratch=[pltpu.SemaphoreType.DMA((NC * parts, quarters))],
    )


def local(hidden, norm_gain, embed_table, tokens, parents, prev_scores, lengths):
    shard = lax.axis_index(VOC)
    core = lax.axis_index("c")
    y = lax.axis_index("y")
    voc_rows, depth = embed_table.shape
    row_count, width = hidden.shape
    scale = math.sqrt(width)
    place = jnp.stack([core, y, lax.axis_index("x")]).astype(jnp.int32)
    gain = norm_gain.reshape(1, width)
    part = row_count // (NC * NX)

    arrived = jnp.stack([tokens] + [shift(tokens, "y", NY, step) for step in (1, 2, 3)])
    pieces, t_cut = cut_pieces(place, hidden, gain, [arrived])
    mine = exchange(pieces, "y")
    other = shift(mine, "c", NC, 1)
    order = (y - jnp.arange(NY)) % NY
    planes = sum(jnp.where((order == s)[:, None], arrived[s : s + 1], 0) for s in range(NY))
    planes = (planes - shard * voc_rows).reshape(NY, NC, NX, part).transpose(1, 2, 0, 3)
    planes = jnp.where(core == 0, planes, planes[::-1]).reshape(NC * NX * NY * part, 1)

    sent, kept, t_pick = pick_rows(planes, embed_table, scale, [t_cut])
    got = shift(sent, "c", NC, 1)
    found, t_found = add(kept, got, [t_pick])
    found = exchange(found.reshape(NX * NY, part, depth), ("x", "y"))
    far_a, far_b, ahead, behind, own, t_far = products(place, mine, other, embed_table, [t_found])
    far_a = shift(far_a, "y", NY, 1)
    far_b = shift(far_b, "y", NY, 3)
    found, _ = sum_rows(found.reshape(NX, NY * part, depth), 1)
    left, right, t_near = add_halves(ahead, behind, far_a, far_b, [])
    left = shift(left, "y", NY, 1)
    right = shift(right, "y", NY, 3)

    found = exchange(found.reshape(NZ, NY * part // NZ, depth), "z")
    spread, t_z = sum_rows(found, NZ)
    spread = exchange(spread, "z").reshape(NY, part, depth)

    states = hidden.astype(jnp.float32)
    meansq = jnp.mean(states * states, axis=-1)
    row_scale = lax.rsqrt(meansq + norm_eps)
    local_col = tokens - shard * voc_rows
    capped, stats, t_cap = cap_and_sum(
        place, own, left, right, row_scale[None], local_col[None], parents[None], [spread]
    )
    stats = exchange(stats, VOC)
    penalty = jnp.power((5.0 + lengths.astype(jnp.float32)) / 6.0, length_power)
    column, chosen_lp, normalized, filler, _ = score(
        stats, parents[None], prev_scores[None], penalty[None], (row_count, voc_rows // 4)
    )
    log_probs = subtract(capped, column)
    late = [shift(array, "c", NC, 1) for array in (left, right)]
    late.append(shift(filler, "c", NC, 1))
    parts = [spread] + [shift(spread, "x", NX, step) for step in (1, 2, 3)]
    next_embed, _ = assemble(place, parts, [shift(piece, "c", NC, 1) for piece in parts], late)
    return (log_probs, chosen_lp[0], normalized[0], next_embed)


def solution(mesh):
    split = Mesh(mesh.devices.reshape(NX, NZ, NC, NY), VOC + ("y",))
    placed = (P("y", None), P(), P(VOC, "y"), P("y"), P("y"), P("y"), P("y"))
    return jax.shard_map(
        local,
        mesh=split,
        in_specs=placed,
        out_specs=(P("y", VOC), P("y"), P("y"), P("y", None)),
        check_vma=False,
    )
```

```python
import math

import jax
import jax.numpy as jnp
from jax import lax
from jax.experimental import pallas as pl
from jax.experimental.pallas import tpu as pltpu
from jax.sharding import Mesh, PartitionSpec as P

BEAMS = 8

soft_cap = 30.0
length_power = 0.6
norm_eps = 1e-06

VOC = ("x", "z", "c")
NX, NZ, NC, NY = 4, 8, 2, 4
BLOCK = 256
CHUNK = 512
SWAP = 512
LANES = 128
VMEM = 36 * 1024 * 1024


def shift(value, axis, size, step):
    return lax.ppermute(value, axis, [(i, (i + step) % size) for i in range(size)])


def exchange(value, axes):
    return lax.all_to_all(value, axes, 0, 0, tiled=True)


def dot_nt(left, right):
    return lax.dot_general(left, right, (((1,), (1,)), ((), ())), preferred_element_type=jnp.float32)


def call(body, outs, args, after=(), smem=0, far_args=0, any_args=0, scratch=()):
    def whole(*refs):
        count = len(args) + len(after)
        tick = refs[count + len(outs)]
        tick[...] = jnp.zeros(tick.shape, tick.dtype)
        body(*refs[: len(args)], *refs[count : count + len(outs)], *refs[count + len(outs) + 1 :])

    spaces = [pltpu.SMEM] * smem + [pltpu.HBM] * far_args + [pl.ANY] * any_args
    spaces += [pltpu.VMEM] * (len(args) - len(spaces)) + [pl.ANY] * len(after)
    args = [
        pltpu.with_memory_space_constraint(arg, pltpu.HBM) if space is pltpu.HBM else arg
        for arg, space in zip(args, spaces)
    ]
    out_specs = []
    for out in outs:
        inside = isinstance(out, jax.ShapeDtypeStruct)
        out_specs.append(pl.BlockSpec(memory_space=pltpu.VMEM if inside else pltpu.HBM))
    return pl.pallas_call(
        whole,
        out_shape=list(outs) + [jax.ShapeDtypeStruct((8, LANES), jnp.float32)],
        in_specs=[pl.BlockSpec(memory_space=space) for space in spaces],
        out_specs=out_specs + [pl.BlockSpec(memory_space=pltpu.VMEM)],
        scratch_shapes=list(scratch),
        cost_estimate=pl.CostEstimate(flops=0, bytes_accessed=0, transcendentals=0),
        compiler_params=pltpu.CompilerParams(vmem_limit_bytes=VMEM),
    )(*args, *after)


def like(shape, dtype=jnp.bfloat16):
    return jax.ShapeDtypeStruct(shape, dtype)


def start_all(copies):
    for copy in copies:
        copy.start()
    return copies


def piece_of(hidden_ref, half, quarter):
    rows, width = hidden_ref.shape
    count, depth = rows // NC, width // NY
    return hidden_ref.at[
        pl.ds(pl.multiple_of(half * count, count), count),
        pl.ds(pl.multiple_of(quarter * depth, LANES), depth),
    ]


def gained(features, gain_ref, quarter):
    depth = features.shape[1]
    gain = gain_ref[:, pl.ds(pl.multiple_of(quarter * depth, LANES), depth)]
    return (features.astype(jnp.float32) * gain.astype(jnp.float32)).astype(features.dtype)


def cut_pieces(place, hidden, gain, after):
    rows, width = hidden.shape
    shape = (NY, rows // NC, width // NY)

    def body(place_ref, hidden_ref, gain_ref, out, held, sems):
        copies = start_all(
            [
                pltpu.make_async_copy(piece_of(hidden_ref, place_ref[0], n), held.at[n], sems.at[n])
                for n in range(NY)
            ]
        )
        for n in range(NY):
            copies[n].wait()
            out[n] = gained(held[n], gain_ref, n)

    return call(
        body, [like(shape)], [place, hidden, gain], after, smem=1, far_args=1,
        scratch=[pltpu.VMEM(shape, hidden.dtype), pltpu.SemaphoreType.DMA((NY,))],
    )


def pick_rows(cols, table, scale, after):
    voc_rows, depth = table.shape
    steps = voc_rows // CHUNK
    count = cols.shape[0] // NC
    blocks = 1
    block = count // blocks

    def body(table_ref, col_ref, sent, kept, held, found, sems):
        load = start_all(
            [
                pltpu.make_async_copy(
                    table_ref.at[n * CHUNK : (n + 1) * CHUNK], held.at[n * CHUNK : (n + 1) * CHUNK], sems.at[n]
                )
                for n in range(steps)
            ]
        )
        put = []
        for n in range(NC * blocks):
            ids = lax.broadcasted_iota(jnp.int32, (block, voc_rows), 1)
            at = (n + blocks) % (NC * blocks) * block
            hot = jnp.where(ids == col_ref[at : at + block], 1.0, 0.0).astype(held.dtype)
            if n == 0:
                for copy in load:
                    copy.wait()
            picked = jnp.dot(hot, held[...], preferred_element_type=jnp.float32)
            found[n] = (picked * scale).astype(found.dtype)
            out = (sent, kept)[n // blocks].at[n % blocks * block : (n % blocks + 1) * block]
            put.append(pltpu.make_async_copy(found.at[n], out, sems.at[steps + n]))
            put[-1].start()
        for copy in put:
            copy.wait()

    return call(
        body, [pltpu.HBM((count, depth), table.dtype)] * 2, [table, cols], after, far_args=1,
        scratch=[
            pltpu.VMEM((voc_rows, depth), table.dtype),
            pltpu.VMEM((NC * blocks, block, depth), table.dtype),
            pltpu.SemaphoreType.DMA((steps + NC * blocks,)),
        ],
    )


def products(place, table, mine, other, distances, splits, after):
    half, depth = mine.shape[1:]
    voc_rows = table.shape[0]
    steps = voc_rows // CHUNK
    rows = NC * half
    count = len(distances)

    def body(place_ref, table_ref, mine_ref, other_ref, *refs):
        outs = refs[: sum(splits)]
        feats, held, results, sems = refs[sum(splits) :]
        load = [
            pltpu.make_async_copy(table_ref.at[n * CHUNK : (n + 1) * CHUNK], held.at[n], sems.at[1, n])
            for n in range(steps)
        ]
        get = []
        for n, distance in enumerate(distances):
            plane = lax.rem(place_ref[1] + distance, NY)
            for k, ref in enumerate((mine_ref, other_ref)):
                start = n * rows + k * half
                get.append(
                    pltpu.make_async_copy(ref.at[plane], feats.at[start : start + half], sems.at[0, NC * n + k])
                )
        start_all(load[:1] + get + load[1:])
        put = []
        for step in range(steps):
            load[step].wait()
            block = held[step].T
            if step == 0:
                for copy in get:
                    copy.wait()
            found = jnp.dot(feats[...], block, preferred_element_type=jnp.float32)
            results[step] = found.astype(results.dtype)
            first = 0
            for n in range(count):
                share = steps // splits[n]
                at = step % share * CHUNK
                out = outs[first + step // share].at[:, at : at + CHUNK]
                piece = results.at[step, n * rows : (n + 1) * rows]
                put.append(pltpu.make_async_copy(piece, out, sems.at[2 + n, step]))
                put[-1].start()
                first += splits[n]
        for copy in put:
            copy.wait()

    kind = table.dtype
    outs = [pltpu.HBM((rows, voc_rows // split), kind) for split in splits for _ in range(split)]
    return call(
        body, outs, [place, table, mine, other], after, smem=1, far_args=1, any_args=2,
        scratch=[
            pltpu.VMEM((count * rows, depth), kind),
            pltpu.VMEM((steps, CHUNK, depth), kind),
            pltpu.VMEM((steps, count * rows, CHUNK), kind),
            pltpu.SemaphoreType.DMA((2 + count, 2 * NY)),
        ],
    )


def scales(hidden, after):
    rows, width = hidden.shape
    steps = rows // LANES

    def body(hidden_ref, out, held, sems):
        load = start_all(
            [
                pltpu.make_async_copy(hidden_ref.at[n * LANES : (n + 1) * LANES], held.at[n], sems.at[n])
                for n in range(steps)
            ]
        )
        for n in range(steps):
            load[n].wait()
            total = jnp.zeros((LANES, LANES), jnp.float32)
            for start in range(0, width, LANES):
                piece = held[n, :, start : start + LANES].astype(jnp.float32)
                total += piece * piece
            mean = jnp.sum(total.T, axis=0, keepdims=True) / width
            out[:, n * LANES : (n + 1) * LANES] = lax.rsqrt(mean + norm_eps)

    return call(
        body, [like((1, rows), jnp.float32)], [hidden], after, far_args=1,
        scratch=[pltpu.VMEM((steps, LANES, width), hidden.dtype), pltpu.SemaphoreType.DMA((steps,))],
    )


def add_halves(ahead, behind, far_a, far_b, after):
    rows, voc_rows = ahead.shape
    wide = voc_rows // 2
    part = rows // NC

    def body(ahead_ref, behind_ref, a_ref, b_ref, left, right, held, sems):
        sides = ((ahead_ref, a_ref, left, 0), (behind_ref, b_ref, right, wide))
        load, put = [], []
        for n, (near, far, out, start) in enumerate(sides):
            for k in range(NC):
                at = slice(k * part, (k + 1) * part)
                load.append(
                    [
                        pltpu.make_async_copy(near.at[at], held.at[n, at], sems.at[n, k]),
                        pltpu.make_async_copy(far.at[at], held.at[2, at, start : start + wide], sems.at[2 + n, k]),
                    ]
                )
                put.append(pltpu.make_async_copy(held.at[n, at], out.at[at], sems.at[4 + n, k]))
        for pair in load:
            start_all(pair)
        for m, pair in enumerate(load):
            n, k = divmod(m, NC)
            for copy in pair:
                copy.wait()
            at, cols = slice(k * part, (k + 1) * part), slice(n * wide, (n + 1) * wide)
            total = held[n, at, cols].astype(jnp.float32) + held[2, at, cols].astype(jnp.float32)
            held[n, at, cols] = total.astype(held.dtype)
            put[m].start()
        for copy in put:
            copy.wait()

    return call(
        body, [pltpu.HBM(ahead.shape, ahead.dtype)] * 2, [ahead, behind, far_a, far_b], after, far_args=2, any_args=2,
        scratch=[pltpu.VMEM((3, rows, voc_rows), ahead.dtype), pltpu.SemaphoreType.DMA((6, NC))],
    )


def cap_and_sum(place, own, left, right, row_scale, cols, parents, after):
    rows, voc_rows = own.shape
    half = rows // NC
    wide = voc_rows // 2

    def body(
        place_ref, own_ref, left_ref, right_ref, scale_ref, col_ref, par_ref, capped_ref, stats_ref,
        held, sems,
    ):
        load = [
            [
                [
                    pltpu.make_async_copy(
                        ref.at[turn * half : (turn + 1) * half, side * wide : (side + 1) * wide],
                        held.at[turn, side, n],
                        sems.at[turn, side, n],
                    )
                    for n, ref in enumerate((own_ref, left_ref, right_ref))
                ]
                for side in range(2)
            ]
            for turn in range(NC)
        ]
        for turn in range(NC):
            for side in range(2):
                start_all(load[turn][side])
        lane = lax.broadcasted_iota(jnp.int32, (half, LANES), 1)
        for turn in range(NC):
            natural = place_ref[0] if turn == 0 else 1 - place_ref[0]
            here = pl.ds(pl.multiple_of(natural * half, half), half)
            scale, col, pick = (
                jnp.broadcast_to(ref[:, here].astype(jnp.float32), (LANES, half)).T
                for ref in (scale_ref, col_ref, par_ref)
            )
            col, pick = col.astype(jnp.int32), pick.astype(jnp.int32)
            total = jnp.zeros((half, LANES), jnp.float32)
            chosen = jnp.zeros((half, LANES), jnp.float32)
            for start in range(0, voc_rows, LANES):
                side = start // wide
                if start % wide == 0:
                    for copy in load[turn][side]:
                        copy.wait()
                at = slice(start % wide, start % wide + LANES)
                logit = sum(held[turn, side, n, :, at].astype(jnp.float32) for n in range(3))
                capped = soft_cap * jnp.tanh(logit * scale / soft_cap)
                capped_ref[here, start : start + LANES] = capped
                total += jnp.exp(capped)
                moved = jnp.concatenate(
                    [
                        jnp.take_along_axis(capped[g : g + BEAMS], pick[g : g + BEAMS], axis=0)
                        for g in range(0, half, BEAMS)
                    ],
                    axis=0,
                )
                chosen += jnp.where(lane + start == col, moved, 0.0)
            for n, part in enumerate((total, chosen)):
                row = jnp.sum(part.T, axis=0, keepdims=True)
                stats_ref[pl.ds(n * NC + natural, 1)] = row
        stats_ref[2 * NC :] = jnp.zeros((SWAP - 2 * NC, half), jnp.float32)

    return call(
        body, [like((rows, voc_rows), jnp.float32), like((SWAP, half), jnp.float32)],
        [place, own, left, right, row_scale, cols, parents], after, smem=1, far_args=3,
        scratch=[pltpu.VMEM((NC, 2, 3, half, wide), own.dtype), pltpu.SemaphoreType.DMA((NC, 2, 3))],
    )


def spread_sum(one, two):
    peers = NX * NZ

    def body(one_ref, two_ref, out):
        total = one_ref[: 2 * NC] + two_ref[: 2 * NC]
        out[...] = jnp.broadcast_to(total[None], out.shape)

    return call(body, [like((peers, 2 * NC, one.shape[1]), one.dtype)], [one, two])


def score(stats, parents, prev_scores, penalty, after):
    rows = parents.shape[1]

    def body(stats_ref, par_ref, prev_ref, pen_ref, column, chosen_ref, norm_ref):
        sums = jnp.sum(stats_ref[...], axis=0)
        lse = jnp.log(sums)
        sub = lax.broadcasted_iota(jnp.int32, (LANES, LANES), 0)
        lane = lax.broadcasted_iota(jnp.int32, (1, LANES), 1)
        for h in range(rows // LANES):
            at = slice(h * LANES, (h + 1) * LANES)

            def down(row):
                return jnp.broadcast_to(row, (LANES, LANES)).T

            lse_col = down(lse[h : h + 1])
            column[at] = lse_col
            hit = sub == lane // BEAMS * BEAMS + par_ref[:, at]
            lse_par = jnp.sum(jnp.where(hit, lse_col, 0.0), axis=0, keepdims=True)
            prev_par = jnp.sum(jnp.where(hit, down(prev_ref[:, at]), 0.0), axis=0, keepdims=True)
            chosen = sums[NC + h : NC + h + 1] - lse_par
            chosen_ref[:, at] = chosen
            norm_ref[:, at] = (prev_par + chosen) / pen_ref[:, at]

    row = like((1, rows), jnp.float32)
    return call(
        body, [like((rows, LANES), jnp.float32), row, row], [stats, parents, prev_scores, penalty], after
    )


def subtract(capped, column):
    rows, voc_rows = capped.shape
    steps = 4

    def body(capped_ref, column_ref, log_ref):
        for start in range(0, voc_rows, LANES):
            at = slice(start, start + LANES)
            log_ref[:, at] = capped_ref[:, at] - column_ref[...]

    block = pl.BlockSpec((rows // steps, voc_rows), lambda i: (i, 0))
    return pl.pallas_call(
        body,
        out_shape=like((rows, voc_rows), jnp.float32),
        grid=(steps,),
        in_specs=[block, pl.BlockSpec((rows // steps, LANES), lambda i: (i, 0))],
        out_specs=block,
        cost_estimate=pl.CostEstimate(flops=0, bytes_accessed=0, transcendentals=0),
        compiler_params=pltpu.CompilerParams(vmem_limit_bytes=VMEM),
    )(capped, column)


def add(one, two, after):
    count, depth = one.shape
    cuts = [slice(start, start + LANES) for start in range(0, count, LANES)]

    def body(one_ref, two_ref, out, held, total, sems):
        load = [
            [
                pltpu.make_async_copy(ref.at[at], held.at[k, at], sems.at[k, n])
                for k, ref in enumerate((one_ref, two_ref))
            ]
            for n, at in enumerate(cuts)
        ]
        put = [pltpu.make_async_copy(total.at[at], out.at[at], sems.at[2, n]) for n, at in enumerate(cuts)]
        for pair in load:
            start_all(pair)
        for n, at in enumerate(cuts):
            for copy in load[n]:
                copy.wait()
            total[at] = held[0, at] + held[1, at]
            put[n].start()
        for copy in put:
            copy.wait()

    return call(
        body, [pltpu.HBM(one.shape, one.dtype)], [one, two], after, far_args=1, any_args=1,
        scratch=[
            pltpu.VMEM((2, *one.shape), one.dtype),
            pltpu.VMEM(one.shape, one.dtype),
            pltpu.SemaphoreType.DMA((3, len(cuts))),
        ],
    )


def sum_rows(stacked, copies, after=()):
    terms, rows, depth = stacked.shape

    def body(in_ref, out):
        found = in_ref[0].astype(jnp.float32)
        for n in range(1, terms):
            found = found + in_ref[n].astype(jnp.float32)
        for n in range(copies):
            out[n] = found.astype(stacked.dtype)

    return call(body, [like((copies, rows, depth))], [stacked], after)


def assemble(place, mine, other):
    parts = len(mine)
    quarters, part, depth = mine[0].shape

    def body(place_ref, *refs):
        *pieces, out, sems = refs
        copies = []
        for n, ref in enumerate(pieces):
            core = place_ref[0] if n < parts else 1 - place_ref[0]
            x = lax.rem(place_ref[2] + parts - n % parts, parts)
            at = pl.ds(pl.multiple_of((core * parts + x) * part, part), part)
            for q in range(quarters):
                copies.append(
                    pltpu.make_async_copy(
                        ref.at[q], out.at[at, q * depth : (q + 1) * depth], sems.at[n, q]
                    )
                )
        start_all(copies)
        for copy in copies:
            copy.wait()

    return call(
        body, [pltpu.HBM((NC * parts * part, quarters * depth), mine[0].dtype)],
        [place, *mine, *other], smem=1,
        scratch=[pltpu.SemaphoreType.DMA((NC * parts, quarters))],
    )


def local(hidden, norm_gain, embed_table, tokens, parents, prev_scores, lengths):
    shard = lax.axis_index(VOC)
    core = lax.axis_index("c")
    y = lax.axis_index("y")
    voc_rows, depth = embed_table.shape
    row_count, width = hidden.shape
    scale = math.sqrt(width)
    place = jnp.stack([core, y, lax.axis_index("x")]).astype(jnp.int32)
    gain = norm_gain.reshape(1, width)
    part = row_count // (NC * NX)

    arrived = [tokens] + [shift(tokens, "y", NY, step) for step in (1, 2, 3)]
    pieces, t_cut = cut_pieces(place, hidden, gain, arrived[1:])
    arrived = jnp.stack(arrived)
    mine = exchange(pieces, "y")
    other = shift(mine, "c", NC, 1)
    order = (y - jnp.arange(NY)) % NY
    planes = sum(jnp.where((order == s)[:, None], arrived[s : s + 1], 0) for s in range(NY))
    planes = (planes - shard * voc_rows).reshape(NY, NC, NX, part).transpose(1, 2, 0, 3)
    planes = jnp.where(core == 0, planes, planes[::-1]).reshape(NC * NX * NY * part, 1)

    sent, kept, t_pick = pick_rows(planes, embed_table, scale, [t_cut])
    got = shift(sent, "c", NC, 1)
    found, t_found = add(kept, got, [t_pick])
    found = exchange(found.reshape(NX * NY, part, depth), ("x", "y"))
    far_a, far_b, t_far = products(place, embed_table, mine, other, (2,), (2,), [t_found])
    far_a = shift(far_a, "y", NY, 1)
    far_b = shift(far_b, "y", NY, 3)
    ahead, behind, own, t_all = products(
        place, embed_table, mine, other, (1, 3, 0), (1, 1, 1), [t_far]
    )
    row_scale, t_scale = scales(hidden, [t_all])
    found, t_sum = sum_rows(found.reshape(NX, NY * part, depth), 1, [t_scale])
    left, right, t_near = add_halves(ahead, behind, far_a, far_b, [t_sum])
    left = shift(left, "y", NY, 1)
    right = shift(right, "y", NY, 3)

    found = exchange(found.reshape(NZ, NY * part // NZ, depth), "z")
    spread, t_z = sum_rows(found, NZ)
    spread = exchange(spread, "z").reshape(NY, part, depth)

    local_col = tokens - shard * voc_rows
    capped, stats, t_cap = cap_and_sum(
        place, own, left, right, row_scale, local_col[None], parents[None], [spread]
    )
    stats, _ = spread_sum(stats, shift(stats, "c", NC, 1))
    stats = exchange(stats, ("x", "z"))
    penalty = jnp.power((5.0 + lengths.astype(jnp.float32)) / 6.0, length_power)
    parts = [spread] + [shift(spread, "x", NX, step) for step in (1, 2, 3)]
    next_embed, t_whole = assemble(place, parts, [shift(piece, "c", NC, 1) for piece in parts])
    column, chosen_lp, normalized, _ = score(
        stats, parents[None], prev_scores[None], penalty[None], [t_whole]
    )
    log_probs = subtract(capped, column)
    return (log_probs, chosen_lp[0], normalized[0], next_embed)


def solution(mesh):
    split = Mesh(mesh.devices.reshape(NX, NZ, NC, NY), VOC + ("y",))
    placed = (P("y", None), P(), P(VOC, "y"), P("y"), P("y"), P("y"), P("y"))
    return jax.shard_map(
        local,
        mesh=split,
        in_specs=placed,
        out_specs=(P("y", VOC), P("y"), P("y"), P("y", None)),
        check_vma=False,
    )
```

```python
import math

import jax
import jax.numpy as jnp
from jax import lax
from jax.experimental import pallas as pl
from jax.experimental.pallas import tpu as pltpu
from jax.sharding import Mesh, PartitionSpec as P

BEAMS = 8

soft_cap = 30.0
length_power = 0.6
norm_eps = 1e-06

VOC = ("x", "z", "c")
NX, NZ, NC, NY = 4, 8, 2, 4
BLOCK = 256
CHUNK = 512
SWAP = 512
LANES = 128
VMEM = 36 * 1024 * 1024


def shift(value, axis, size, step):
    return lax.ppermute(value, axis, [(i, (i + step) % size) for i in range(size)])


def exchange(value, axes):
    return lax.all_to_all(value, axes, 0, 0, tiled=True)


def dot_nt(left, right):
    return lax.dot_general(left, right, (((1,), (1,)), ((), ())), preferred_element_type=jnp.float32)


def call(body, outs, args, after=(), smem=0, far_args=0, any_args=0, scratch=()):
    def whole(*refs):
        count = len(args) + len(after)
        tick = refs[count + len(outs)]
        tick[...] = jnp.zeros(tick.shape, tick.dtype)
        body(*refs[: len(args)], *refs[count : count + len(outs)], *refs[count + len(outs) + 1 :])

    spaces = [pltpu.SMEM] * smem + [pltpu.HBM] * far_args + [pl.ANY] * any_args
    spaces += [pltpu.VMEM] * (len(args) - len(spaces)) + [pl.ANY] * len(after)
    args = [
        pltpu.with_memory_space_constraint(arg, pltpu.HBM) if space is pltpu.HBM else arg
        for arg, space in zip(args, spaces)
    ]
    out_specs = []
    for out in outs:
        inside = isinstance(out, jax.ShapeDtypeStruct)
        out_specs.append(pl.BlockSpec(memory_space=pltpu.VMEM if inside else pltpu.HBM))
    return pl.pallas_call(
        whole,
        out_shape=list(outs) + [jax.ShapeDtypeStruct((8, LANES), jnp.float32)],
        in_specs=[pl.BlockSpec(memory_space=space) for space in spaces],
        out_specs=out_specs + [pl.BlockSpec(memory_space=pltpu.VMEM)],
        scratch_shapes=list(scratch),
        cost_estimate=pl.CostEstimate(flops=0, bytes_accessed=0, transcendentals=0),
        compiler_params=pltpu.CompilerParams(vmem_limit_bytes=VMEM),
    )(*args, *after)


def like(shape, dtype=jnp.bfloat16):
    return jax.ShapeDtypeStruct(shape, dtype)


def start_all(copies):
    for copy in copies:
        copy.start()
    return copies


def piece_of(hidden_ref, half, quarter):
    rows, width = hidden_ref.shape
    count, depth = rows // NC, width // NY
    return hidden_ref.at[
        pl.ds(pl.multiple_of(half * count, count), count),
        pl.ds(pl.multiple_of(quarter * depth, LANES), depth),
    ]


def gained(features, gain_ref, quarter):
    depth = features.shape[1]
    gain = gain_ref[:, pl.ds(pl.multiple_of(quarter * depth, LANES), depth)]
    return (features.astype(jnp.float32) * gain.astype(jnp.float32)).astype(features.dtype)


def cut_pieces(place, hidden, gain, after):
    rows, width = hidden.shape
    shape = (NY, rows // NC, width // NY)

    def body(place_ref, hidden_ref, gain_ref, out, held, sems):
        copies = start_all(
            [
                pltpu.make_async_copy(piece_of(hidden_ref, place_ref[0], n), held.at[n], sems.at[n])
                for n in range(NY)
            ]
        )
        for n in range(NY):
            copies[n].wait()
            out[n] = gained(held[n], gain_ref, n)

    return call(
        body, [like(shape)], [place, hidden, gain], after, smem=1, far_args=1,
        scratch=[pltpu.VMEM(shape, hidden.dtype), pltpu.SemaphoreType.DMA((NY,))],
    )


def pick_rows(cols, table, scale, after):
    voc_rows, depth = table.shape
    steps = voc_rows // CHUNK
    count = cols.shape[0] // NC
    blocks = 1
    block = count // blocks

    def body(table_ref, col_ref, sent, kept, held, found, sems):
        load = start_all(
            [
                pltpu.make_async_copy(
                    table_ref.at[n * CHUNK : (n + 1) * CHUNK], held.at[n * CHUNK : (n + 1) * CHUNK], sems.at[n]
                )
                for n in range(steps)
            ]
        )
        put = []
        for n in range(NC * blocks):
            ids = lax.broadcasted_iota(jnp.int32, (block, voc_rows), 1)
            at = (n + blocks) % (NC * blocks) * block
            hot = jnp.where(ids == col_ref[at : at + block], 1.0, 0.0).astype(held.dtype)
            if n == 0:
                for copy in load:
                    copy.wait()
            picked = jnp.dot(hot, held[...], preferred_element_type=jnp.float32)
            found[n] = (picked * scale).astype(found.dtype)
            out = (sent, kept)[n // blocks].at[n % blocks * block : (n % blocks + 1) * block]
            put.append(pltpu.make_async_copy(found.at[n], out, sems.at[steps + n]))
            put[-1].start()
        for copy in put:
            copy.wait()

    return call(
        body, [pltpu.HBM((count, depth), table.dtype)] * 2, [table, cols], after, far_args=1,
        scratch=[
            pltpu.VMEM((voc_rows, depth), table.dtype),
            pltpu.VMEM((NC * blocks, block, depth), table.dtype),
            pltpu.SemaphoreType.DMA((steps + NC * blocks,)),
        ],
    )


def products(place, table, mine, other, distances, splits, after):
    half, depth = mine.shape[1:]
    voc_rows = table.shape[0]
    steps = voc_rows // CHUNK
    rows = NC * half
    count = len(distances)

    def body(place_ref, table_ref, mine_ref, other_ref, *refs):
        outs = refs[: sum(splits)]
        feats, held, results, sems = refs[sum(splits) :]
        load = [
            pltpu.make_async_copy(table_ref.at[n * CHUNK : (n + 1) * CHUNK], held.at[n], sems.at[1, n])
            for n in range(steps)
        ]
        get = []
        for n, distance in enumerate(distances):
            plane = lax.rem(place_ref[1] + distance, NY)
            for k, ref in enumerate((mine_ref, other_ref)):
                start = n * rows + k * half
                get.append(
                    pltpu.make_async_copy(ref.at[plane], feats.at[start : start + half], sems.at[0, NC * n + k])
                )
        start_all(load[:1] + get + load[1:])
        put = []
        for step in range(steps):
            load[step].wait()
            block = held[step].T
            if step == 0:
                for copy in get:
                    copy.wait()
            found = jnp.dot(feats[...], block, preferred_element_type=jnp.float32)
            results[step] = found.astype(results.dtype)
            first = 0
            for n in range(count):
                share = steps // splits[n]
                at = step % share * CHUNK
                out = outs[first + step // share].at[:, at : at + CHUNK]
                piece = results.at[step, n * rows : (n + 1) * rows]
                put.append(pltpu.make_async_copy(piece, out, sems.at[2 + n, step]))
                put[-1].start()
                first += splits[n]
        for copy in put:
            copy.wait()

    kind = table.dtype
    outs = [pltpu.HBM((rows, voc_rows // split), kind) for split in splits for _ in range(split)]
    return call(
        body, outs, [place, table, mine, other], after, smem=1, far_args=1, any_args=2,
        scratch=[
            pltpu.VMEM((count * rows, depth), kind),
            pltpu.VMEM((steps, CHUNK, depth), kind),
            pltpu.VMEM((steps, count * rows, CHUNK), kind),
            pltpu.SemaphoreType.DMA((2 + count, 2 * NY)),
        ],
    )


def scales(hidden, after):
    rows, width = hidden.shape
    steps = rows // LANES

    def body(hidden_ref, out, held, sems):
        load = start_all(
            [
                pltpu.make_async_copy(hidden_ref.at[n * LANES : (n + 1) * LANES], held.at[n], sems.at[n])
                for n in range(steps)
            ]
        )
        for n in range(steps):
            load[n].wait()
            total = jnp.zeros((LANES, LANES), jnp.float32)
            for start in range(0, width, LANES):
                piece = held[n, :, start : start + LANES].astype(jnp.float32)
                total += piece * piece
            mean = jnp.sum(total.T, axis=0, keepdims=True) / width
            out[:, n * LANES : (n + 1) * LANES] = lax.rsqrt(mean + norm_eps)

    return call(
        body, [like((1, rows), jnp.float32)], [hidden], after, far_args=1,
        scratch=[pltpu.VMEM((steps, LANES, width), hidden.dtype), pltpu.SemaphoreType.DMA((steps,))],
    )


def add_halves(ahead, behind, far_a, far_b, after):
    rows, voc_rows = ahead.shape
    wide = voc_rows // 2
    part = rows // NC

    def body(ahead_ref, behind_ref, a_ref, b_ref, left, right, held, sems):
        sides = ((ahead_ref, a_ref, left, 0), (behind_ref, b_ref, right, wide))
        load, put = [], []
        for n, (near, far, out, start) in enumerate(sides):
            for k in range(NC):
                at = slice(k * part, (k + 1) * part)
                load.append(
                    [
                        pltpu.make_async_copy(near.at[at], held.at[n, at], sems.at[n, k]),
                        pltpu.make_async_copy(far.at[at], held.at[2, at, start : start + wide], sems.at[2 + n, k]),
                    ]
                )
                put.append(pltpu.make_async_copy(held.at[n, at], out.at[at], sems.at[4 + n, k]))
        for pair in load:
            start_all(pair)
        for m, pair in enumerate(load):
            n, k = divmod(m, NC)
            for copy in pair:
                copy.wait()
            at, cols = slice(k * part, (k + 1) * part), slice(n * wide, (n + 1) * wide)
            total = held[n, at, cols].astype(jnp.float32) + held[2, at, cols].astype(jnp.float32)
            held[n, at, cols] = total.astype(held.dtype)
            put[m].start()
        for copy in put:
            copy.wait()

    return call(
        body, [pltpu.HBM(ahead.shape, ahead.dtype)] * 2, [ahead, behind, far_a, far_b], after, far_args=2, any_args=2,
        scratch=[pltpu.VMEM((3, rows, voc_rows), ahead.dtype), pltpu.SemaphoreType.DMA((6, NC))],
    )


def cap_and_sum(place, own, left, right, row_scale, cols, parents, after):
    rows, voc_rows = own.shape
    half = rows // NC
    wide = voc_rows // 2

    def body(
        place_ref, own_ref, left_ref, right_ref, scale_ref, col_ref, par_ref, capped_ref, stats_ref,
        held, sems,
    ):
        load = [
            [
                [
                    pltpu.make_async_copy(
                        ref.at[turn * half : (turn + 1) * half, side * wide : (side + 1) * wide],
                        held.at[turn, side, n],
                        sems.at[turn, side, n],
                    )
                    for n, ref in enumerate((own_ref, left_ref, right_ref))
                ]
                for side in range(2)
            ]
            for turn in range(NC)
        ]
        for turn in range(NC):
            for side in range(2):
                start_all(load[turn][side])
        lane = lax.broadcasted_iota(jnp.int32, (half, LANES), 1)
        for turn in range(NC):
            natural = place_ref[0] if turn == 0 else 1 - place_ref[0]
            here = pl.ds(pl.multiple_of(natural * half, half), half)
            scale, col, pick = (
                jnp.broadcast_to(ref[:, here].astype(jnp.float32), (LANES, half)).T
                for ref in (scale_ref, col_ref, par_ref)
            )
            col, pick = col.astype(jnp.int32), pick.astype(jnp.int32)
            total = jnp.zeros((half, LANES), jnp.float32)
            chosen = jnp.zeros((half, LANES), jnp.float32)
            for start in range(0, voc_rows, LANES):
                side = start // wide
                if start % wide == 0:
                    for copy in load[turn][side]:
                        copy.wait()
                at = slice(start % wide, start % wide + LANES)
                logit = sum(held[turn, side, n, :, at].astype(jnp.float32) for n in range(3))
                capped = soft_cap * jnp.tanh(logit * scale / soft_cap)
                capped_ref[here, start : start + LANES] = capped
                total += jnp.exp(capped)
                moved = jnp.concatenate(
                    [
                        jnp.take_along_axis(capped[g : g + BEAMS], pick[g : g + BEAMS], axis=0)
                        for g in range(0, half, BEAMS)
                    ],
                    axis=0,
                )
                chosen += jnp.where(lane + start == col, moved, 0.0)
            for n, part in enumerate((total, chosen)):
                row = jnp.sum(part.T, axis=0, keepdims=True)
                stats_ref[pl.ds(n * NC + natural, 1)] = row
        stats_ref[2 * NC :] = jnp.zeros((SWAP - 2 * NC, half), jnp.float32)

    return call(
        body, [like((rows, voc_rows), jnp.float32), like((SWAP, half), jnp.float32)],
        [place, own, left, right, row_scale, cols, parents], after, smem=1, far_args=3,
        scratch=[pltpu.VMEM((NC, 2, 3, half, wide), own.dtype), pltpu.SemaphoreType.DMA((NC, 2, 3))],
    )


def spread_sum(one, two):
    peers = NX * NZ

    def body(one_ref, two_ref, out):
        total = one_ref[: 2 * NC] + two_ref[: 2 * NC]
        out[...] = jnp.broadcast_to(total[None], out.shape)

    return call(body, [like((peers, 2 * NC, one.shape[1]), one.dtype)], [one, two])


def finish(capped, stats, parents, prev_scores, penalty, after):
    rows, voc_rows = capped.shape
    steps = 4
    part = rows // steps

    def body(capped_ref, stats_ref, par_ref, prev_ref, pen_ref, after_ref, log_ref, chosen_ref, norm_ref, column):
        step = pl.program_id(0)

        @pl.when(step == 0)
        def _():
            sums = jnp.sum(stats_ref[...], axis=0)
            lse = jnp.log(sums)
            sub = lax.broadcasted_iota(jnp.int32, (LANES, LANES), 0)
            lane = lax.broadcasted_iota(jnp.int32, (1, LANES), 1)
            for h in range(rows // LANES):
                at = slice(h * LANES, (h + 1) * LANES)

                def down(row):
                    return jnp.broadcast_to(row, (LANES, LANES)).T

                lse_col = down(lse[h : h + 1])
                column[at] = lse_col
                hit = sub == lane // BEAMS * BEAMS + par_ref[:, at]
                lse_par = jnp.sum(jnp.where(hit, lse_col, 0.0), axis=0, keepdims=True)
                prev_par = jnp.sum(jnp.where(hit, down(prev_ref[:, at]), 0.0), axis=0, keepdims=True)
                chosen = sums[NC + h : NC + h + 1] - lse_par
                chosen_ref[:, at] = chosen
                norm_ref[:, at] = (prev_par + chosen) / pen_ref[:, at]

        lse_here = column[pl.ds(pl.multiple_of(step * part, part), part)]
        for start in range(0, voc_rows, LANES):
            at = slice(start, start + LANES)
            log_ref[:, at] = capped_ref[:, at] - lse_here

    block = pl.BlockSpec((part, voc_rows), lambda i: (i, 0))
    row = pl.BlockSpec((1, rows), lambda i: (0, 0))
    return pl.pallas_call(
        body,
        out_shape=[
            like((rows, voc_rows), jnp.float32), like((1, rows), jnp.float32), like((1, rows), jnp.float32)
        ],
        grid=(steps,),
        in_specs=[
            block, pl.BlockSpec(stats.shape, lambda i: (0, 0, 0)), row, row, row,
            pl.BlockSpec(memory_space=pl.ANY),
        ],
        out_specs=[block, row, row],
        scratch_shapes=[pltpu.VMEM((rows, LANES), jnp.float32)],
        cost_estimate=pl.CostEstimate(flops=0, bytes_accessed=0, transcendentals=0),
        compiler_params=pltpu.CompilerParams(vmem_limit_bytes=VMEM),
    )(capped, stats, parents, prev_scores, penalty, after)


def add(one, two, after):
    count, depth = one.shape
    cuts = [slice(start, start + LANES) for start in range(0, count, LANES)]

    def body(one_ref, two_ref, out, held, total, sems):
        load = [
            [
                pltpu.make_async_copy(ref.at[at], held.at[k, at], sems.at[k, n])
                for k, ref in enumerate((one_ref, two_ref))
            ]
            for n, at in enumerate(cuts)
        ]
        put = [pltpu.make_async_copy(total.at[at], out.at[at], sems.at[2, n]) for n, at in enumerate(cuts)]
        for pair in load:
            start_all(pair)
        for n, at in enumerate(cuts):
            for copy in load[n]:
                copy.wait()
            total[at] = held[0, at] + held[1, at]
            put[n].start()
        for copy in put:
            copy.wait()

    return call(
        body, [pltpu.HBM(one.shape, one.dtype)], [one, two], after, far_args=1, any_args=1,
        scratch=[
            pltpu.VMEM((2, *one.shape), one.dtype),
            pltpu.VMEM(one.shape, one.dtype),
            pltpu.SemaphoreType.DMA((3, len(cuts))),
        ],
    )


def sum_rows(stacked, copies, after=()):
    terms, rows, depth = stacked.shape

    def body(in_ref, out):
        found = in_ref[0].astype(jnp.float32)
        for n in range(1, terms):
            found = found + in_ref[n].astype(jnp.float32)
        for n in range(copies):
            out[n] = found.astype(stacked.dtype)

    return call(body, [like((copies, rows, depth))], [stacked], after)


def assemble(place, mine, other):
    parts = len(mine)
    quarters, part, depth = mine[0].shape

    def body(place_ref, *refs):
        *pieces, out, sems = refs
        copies = []
        for n, ref in enumerate(pieces):
            core = place_ref[0] if n < parts else 1 - place_ref[0]
            x = lax.rem(place_ref[2] + parts - n % parts, parts)
            at = pl.ds(pl.multiple_of((core * parts + x) * part, part), part)
            for q in range(quarters):
                copies.append(
                    pltpu.make_async_copy(
                        ref.at[q], out.at[at, q * depth : (q + 1) * depth], sems.at[n, q]
                    )
                )
        start_all(copies)
        for copy in copies:
            copy.wait()

    return call(
        body, [pltpu.HBM((NC * parts * part, quarters * depth), mine[0].dtype)],
        [place, *mine, *other], smem=1,
        scratch=[pltpu.SemaphoreType.DMA((NC * parts, quarters))],
    )


def local(hidden, norm_gain, embed_table, tokens, parents, prev_scores, lengths):
    shard = lax.axis_index(VOC)
    core = lax.axis_index("c")
    y = lax.axis_index("y")
    voc_rows, depth = embed_table.shape
    row_count, width = hidden.shape
    scale = math.sqrt(width)
    place = jnp.stack([core, y, lax.axis_index("x")]).astype(jnp.int32)
    gain = norm_gain.reshape(1, width)
    part = row_count // (NC * NX)

    arrived = [tokens] + [shift(tokens, "y", NY, step) for step in (1, 2, 3)]
    pieces, t_cut = cut_pieces(place, hidden, gain, arrived[1:])
    arrived = jnp.stack(arrived)
    mine = exchange(pieces, "y")
    other = shift(mine, "c", NC, 1)
    order = (y - jnp.arange(NY)) % NY
    planes = sum(jnp.where((order == s)[:, None], arrived[s : s + 1], 0) for s in range(NY))
    planes = (planes - shard * voc_rows).reshape(NY, NC, NX, part).transpose(1, 2, 0, 3)
    planes = jnp.where(core == 0, planes, planes[::-1]).reshape(NC * NX * NY * part, 1)

    sent, kept, t_pick = pick_rows(planes, embed_table, scale, [t_cut])
    got = shift(sent, "c", NC, 1)
    found, t_found = add(kept, got, [t_pick])
    found = exchange(found.reshape(NX * NY, part, depth), ("x", "y"))
    far_a, far_b, t_far = products(place, embed_table, mine, other, (2,), (2,), [t_found])
    far_a = shift(far_a, "y", NY, 1)
    far_b = shift(far_b, "y", NY, 3)
    ahead, behind, own, t_all = products(
        place, embed_table, mine, other, (1, 3, 0), (1, 1, 1), [t_far]
    )
    row_scale, t_scale = scales(hidden, [t_all])
    found, t_sum = sum_rows(found.reshape(NX, NY * part, depth), 1, [t_scale])
    left, right, t_near = add_halves(ahead, behind, far_a, far_b, [t_sum])
    left = shift(left, "y", NY, 1)
    right = shift(right, "y", NY, 3)

    found = exchange(found.reshape(NZ, NY * part // NZ, depth), "z")
    spread, t_z = sum_rows(found, NZ)
    spread = exchange(spread, "z").reshape(NY, part, depth)

    local_col = tokens - shard * voc_rows
    capped, stats, t_cap = cap_and_sum(
        place, own, left, right, row_scale, local_col[None], parents[None], [spread]
    )
    stats, _ = spread_sum(stats, shift(stats, "c", NC, 1))
    stats = exchange(stats, ("x", "z"))
    penalty = jnp.power((5.0 + lengths.astype(jnp.float32)) / 6.0, length_power)
    parts = [spread] + [shift(spread, "x", NX, step) for step in (1, 2, 3)]
    next_embed, t_whole = assemble(place, parts, [shift(piece, "c", NC, 1) for piece in parts])
    log_probs, chosen_lp, normalized = finish(
        capped, stats, parents[None], prev_scores[None], penalty[None], t_whole
    )
    return (log_probs, chosen_lp[0], normalized[0], next_embed)


def solution(mesh):
    split = Mesh(mesh.devices.reshape(NX, NZ, NC, NY), VOC + ("y",))
    placed = (P("y", None), P(), P(VOC, "y"), P("y"), P("y"), P("y"), P("y"))
    return jax.shard_map(
        local,
        mesh=split,
        in_specs=placed,
        out_specs=(P("y", VOC), P("y"), P("y"), P("y", None)),
        check_vma=False,
    )
```

```python
import math

import jax
import jax.numpy as jnp
from jax import lax
from jax.experimental import pallas as pl
from jax.experimental.pallas import tpu as pltpu
from jax.sharding import Mesh, PartitionSpec as P

BEAMS = 8

soft_cap = 30.0
length_power = 0.6
norm_eps = 1e-06

VOC = ("x", "z", "c")
NX, NZ, NC, NY = 4, 8, 2, 4
BLOCK = 256
CHUNK = 512
SWAP = 512
LANES = 128
VMEM = 36 * 1024 * 1024


def shift(value, axis, size, step):
    return lax.ppermute(value, axis, [(i, (i + step) % size) for i in range(size)])


def exchange(value, axes):
    return lax.all_to_all(value, axes, 0, 0, tiled=True)


def dot_nt(left, right):
    return lax.dot_general(left, right, (((1,), (1,)), ((), ())), preferred_element_type=jnp.float32)


def call(body, outs, args, after=(), smem=0, far_args=0, any_args=0, scratch=()):
    def whole(*refs):
        count = len(args) + len(after)
        tick = refs[count + len(outs)]
        tick[...] = jnp.zeros(tick.shape, tick.dtype)
        body(*refs[: len(args)], *refs[count : count + len(outs)], *refs[count + len(outs) + 1 :])

    spaces = [pltpu.SMEM] * smem + [pltpu.HBM] * far_args + [pl.ANY] * any_args
    spaces += [pltpu.VMEM] * (len(args) - len(spaces)) + [pl.ANY] * len(after)
    args = [
        pltpu.with_memory_space_constraint(arg, pltpu.HBM) if space is pltpu.HBM else arg
        for arg, space in zip(args, spaces)
    ]
    out_specs = []
    for out in outs:
        inside = isinstance(out, jax.ShapeDtypeStruct)
        out_specs.append(pl.BlockSpec(memory_space=pltpu.VMEM if inside else pltpu.HBM))
    return pl.pallas_call(
        whole,
        out_shape=list(outs) + [jax.ShapeDtypeStruct((8, LANES), jnp.float32)],
        in_specs=[pl.BlockSpec(memory_space=space) for space in spaces],
        out_specs=out_specs + [pl.BlockSpec(memory_space=pltpu.VMEM)],
        scratch_shapes=list(scratch),
        cost_estimate=pl.CostEstimate(flops=0, bytes_accessed=0, transcendentals=0),
        compiler_params=pltpu.CompilerParams(vmem_limit_bytes=VMEM),
    )(*args, *after)


def like(shape, dtype=jnp.bfloat16):
    return jax.ShapeDtypeStruct(shape, dtype)


def start_all(copies):
    for copy in copies:
        copy.start()
    return copies


def piece_of(hidden_ref, half, quarter):
    rows, width = hidden_ref.shape
    count, depth = rows // NC, width // NY
    return hidden_ref.at[
        pl.ds(pl.multiple_of(half * count, count), count),
        pl.ds(pl.multiple_of(quarter * depth, LANES), depth),
    ]


def gained(features, gain_ref, quarter):
    depth = features.shape[1]
    gain = gain_ref[:, pl.ds(pl.multiple_of(quarter * depth, LANES), depth)]
    return (features.astype(jnp.float32) * gain.astype(jnp.float32)).astype(features.dtype)


def cut_pieces(place, hidden, gain, after):
    rows, width = hidden.shape
    shape = (NY, rows // NC, width // NY)

    def body(place_ref, hidden_ref, gain_ref, out, held, sems):
        copies = start_all(
            [
                pltpu.make_async_copy(piece_of(hidden_ref, place_ref[0], n), held.at[n], sems.at[n])
                for n in range(NY)
            ]
        )
        for n in range(NY):
            copies[n].wait()
            out[n] = gained(held[n], gain_ref, n)

    return call(
        body, [like(shape)], [place, hidden, gain], after, smem=1, far_args=1,
        scratch=[pltpu.VMEM(shape, hidden.dtype), pltpu.SemaphoreType.DMA((NY,))],
    )


def take_planes(place, mine, groups):
    def body(place_ref, mine_ref, *refs):
        copies = []
        for out, distances in zip(refs, groups):
            for n, distance in enumerate(distances):
                plane = lax.rem(place_ref[1] + distance, NY)
                copies.append(pltpu.make_async_copy(mine_ref.at[plane], out.at[n], refs[-1].at[len(copies)]))
        for copy in start_all(copies):
            copy.wait()

    outs = [like((len(distances), *mine.shape[1:])) for distances in groups]
    return call(
        body, outs, [place, mine], smem=1, any_args=1, scratch=[pltpu.SemaphoreType.DMA((NY,))]
    )


def pick_rows(cols, table, scale, after):
    voc_rows, depth = table.shape
    steps = voc_rows // CHUNK
    count = cols.shape[0] // NC
    blocks = 1
    block = count // blocks

    def body(table_ref, col_ref, sent_a, sent_b, kept, held, found, sems):
        load = start_all(
            [
                pltpu.make_async_copy(
                    table_ref.at[n * CHUNK : (n + 1) * CHUNK], held.at[n * CHUNK : (n + 1) * CHUNK], sems.at[n]
                )
                for n in range(steps)
            ]
        )
        put = []
        for n in range(NC * blocks):
            ids = lax.broadcasted_iota(jnp.int32, (block, voc_rows), 1)
            at = (n + blocks) % (NC * blocks) * block
            hot = jnp.where(ids == col_ref[at : at + block], 1.0, 0.0).astype(held.dtype)
            if n == 0:
                for copy in load:
                    copy.wait()
            picked = jnp.dot(hot, held[...], preferred_element_type=jnp.float32)
            found[n] = (picked * scale).astype(found.dtype)
            if n == 0:
                parts = ((found.at[0, : block // 2], sent_a), (found.at[0, block // 2 :], sent_b))
            else:
                parts = ((found.at[n], kept),)
            for part, out in parts:
                put.append(pltpu.make_async_copy(part, out, sems.at[steps + len(put)]))
                put[-1].start()
        for copy in put:
            copy.wait()

    return call(
        body, [pltpu.HBM((rows, depth), table.dtype) for rows in (count // 2, count // 2, count)], [table, cols], after, far_args=1,
        scratch=[
            pltpu.VMEM((voc_rows, depth), table.dtype),
            pltpu.VMEM((NC * blocks, block, depth), table.dtype),
            pltpu.SemaphoreType.DMA((steps + 3,)),
        ],
    )


def products(place, table, mine, others, distances, splits, after):
    half, depth = mine.shape[1:]
    voc_rows = table.shape[0]
    steps = voc_rows // CHUNK
    rows = NC * half
    count = len(distances)

    def body(place_ref, table_ref, mine_ref, *refs):
        outs = refs[len(others) : -4]
        feats, held, results, sems = refs[-4:]
        load = [
            pltpu.make_async_copy(table_ref.at[n * CHUNK : (n + 1) * CHUNK], held.at[n], sems.at[1, n])
            for n in range(steps)
        ]
        get = []
        for n, distance in enumerate(distances):
            plane = lax.rem(place_ref[1] + distance, NY)
            for k, ref in enumerate((mine_ref.at[plane], refs[1 - distance // 2].at[distance % 2])):
                start = n * rows + k * half
                get.append(
                    pltpu.make_async_copy(ref, feats.at[start : start + half], sems.at[0, NC * n + k])
                )
        start_all(load[:1] + get + load[1:])
        put = []
        for step in range(steps):
            load[step].wait()
            block = held[step].T
            if step == 0:
                for copy in get:
                    copy.wait()
            found = jnp.dot(feats[...], block, preferred_element_type=jnp.float32)
            results[step] = found.astype(results.dtype)
            first = 0
            for n in range(count):
                share = steps // splits[n]
                at = step % share * CHUNK
                out = outs[first + step // share].at[:, at : at + CHUNK]
                piece = results.at[step, n * rows : (n + 1) * rows]
                put.append(pltpu.make_async_copy(piece, out, sems.at[2 + n, step]))
                put[-1].start()
                first += splits[n]
        for copy in put:
            copy.wait()

    kind = table.dtype
    outs = [pltpu.HBM((rows, voc_rows // split), kind) for split in splits for _ in range(split)]
    return call(
        body, outs, [place, table, mine, *others], after, smem=1, far_args=1, any_args=1 + len(others),
        scratch=[
            pltpu.VMEM((count * rows, depth), kind),
            pltpu.VMEM((steps, CHUNK, depth), kind),
            pltpu.VMEM((steps, count * rows, CHUNK), kind),
            pltpu.SemaphoreType.DMA((2 + count, 2 * NY)),
        ],
    )


def scales(hidden, after):
    rows, width = hidden.shape
    steps = rows // LANES

    def body(hidden_ref, out, held, sems):
        load = start_all(
            [
                pltpu.make_async_copy(hidden_ref.at[n * LANES : (n + 1) * LANES], held.at[n], sems.at[n])
                for n in range(steps)
            ]
        )
        for n in range(steps):
            load[n].wait()
            total = jnp.zeros((LANES, LANES), jnp.float32)
            for start in range(0, width, LANES):
                piece = held[n, :, start : start + LANES].astype(jnp.float32)
                total += piece * piece
            mean = jnp.sum(total.T, axis=0, keepdims=True) / width
            out[:, n * LANES : (n + 1) * LANES] = lax.rsqrt(mean + norm_eps)

    return call(
        body, [like((1, rows), jnp.float32)], [hidden], after, far_args=1,
        scratch=[pltpu.VMEM((steps, LANES, width), hidden.dtype), pltpu.SemaphoreType.DMA((steps,))],
    )


def add_halves(ahead, behind, far_a, far_b, after):
    rows, voc_rows = ahead.shape
    wide = voc_rows // 2
    part = rows // NC

    def body(ahead_ref, behind_ref, a_ref, b_ref, left, right, held, sems):
        sides = ((ahead_ref, a_ref, left, 0), (behind_ref, b_ref, right, wide))
        load, put = [], []
        for n, (near, far, out, start) in enumerate(sides):
            for k in range(NC):
                at = slice(k * part, (k + 1) * part)
                load.append(
                    [
                        pltpu.make_async_copy(near.at[at], held.at[n, at], sems.at[n, k]),
                        pltpu.make_async_copy(far.at[at], held.at[2, at, start : start + wide], sems.at[2 + n, k]),
                    ]
                )
                put.append(pltpu.make_async_copy(held.at[n, at], out.at[at], sems.at[4 + n, k]))
        for pair in load:
            start_all(pair)
        for m, pair in enumerate(load):
            n, k = divmod(m, NC)
            for copy in pair:
                copy.wait()
            at, cols = slice(k * part, (k + 1) * part), slice(n * wide, (n + 1) * wide)
            total = held[n, at, cols].astype(jnp.float32) + held[2, at, cols].astype(jnp.float32)
            held[n, at, cols] = total.astype(held.dtype)
            put[m].start()
        for copy in put:
            copy.wait()

    return call(
        body, [pltpu.HBM(ahead.shape, ahead.dtype)] * 2, [ahead, behind, far_a, far_b], after, far_args=2, any_args=2,
        scratch=[pltpu.VMEM((3, rows, voc_rows), ahead.dtype), pltpu.SemaphoreType.DMA((6, NC))],
    )


def cap_and_sum(place, own, left, right, row_scale, cols, parents, after):
    rows, voc_rows = own.shape
    half = rows // NC
    wide = voc_rows // 2

    def body(
        place_ref, own_ref, left_ref, right_ref, scale_ref, col_ref, par_ref, capped_ref, stats_ref,
        held, sems,
    ):
        load = [
            [
                [
                    pltpu.make_async_copy(
                        ref.at[turn * half : (turn + 1) * half, side * wide : (side + 1) * wide],
                        held.at[turn, side, n],
                        sems.at[turn, side, n],
                    )
                    for n, ref in enumerate((own_ref, left_ref, right_ref))
                ]
                for side in range(2)
            ]
            for turn in range(NC)
        ]
        for turn in range(NC):
            for side in range(2):
                start_all(load[turn][side])
        lane = lax.broadcasted_iota(jnp.int32, (half, LANES), 1)
        for turn in range(NC):
            natural = place_ref[0] if turn == 0 else 1 - place_ref[0]
            here = pl.ds(pl.multiple_of(natural * half, half), half)
            scale, col, pick = (
                jnp.broadcast_to(ref[:, here].astype(jnp.float32), (LANES, half)).T
                for ref in (scale_ref, col_ref, par_ref)
            )
            col, pick = col.astype(jnp.int32), pick.astype(jnp.int32)
            total = jnp.zeros((half, LANES), jnp.float32)
            chosen = jnp.zeros((half, LANES), jnp.float32)
            for start in range(0, voc_rows, LANES):
                side = start // wide
                if start % wide == 0:
                    for copy in load[turn][side]:
                        copy.wait()
                at = slice(start % wide, start % wide + LANES)
                logit = sum(held[turn, side, n, :, at].astype(jnp.float32) for n in range(3))
                capped = soft_cap * jnp.tanh(logit * scale / soft_cap)
                capped_ref[here, start : start + LANES] = capped
                total += jnp.exp(capped)
                moved = jnp.concatenate(
                    [
                        jnp.take_along_axis(capped[g : g + BEAMS], pick[g : g + BEAMS], axis=0)
                        for g in range(0, half, BEAMS)
                    ],
                    axis=0,
                )
                chosen += jnp.where(lane + start == col, moved, 0.0)
            for n, part in enumerate((total, chosen)):
                row = jnp.sum(part.T, axis=0, keepdims=True)
                stats_ref[pl.ds(n * NC + natural, 1)] = row
        stats_ref[2 * NC :] = jnp.zeros((SWAP - 2 * NC, half), jnp.float32)

    return call(
        body, [like((rows, voc_rows), jnp.float32), like((SWAP, half), jnp.float32)],
        [place, own, left, right, row_scale, cols, parents], after, smem=1, far_args=3,
        scratch=[pltpu.VMEM((NC, 2, 3, half, wide), own.dtype), pltpu.SemaphoreType.DMA((NC, 2, 3))],
    )


def spread_sum(one, two):
    peers = NX * NZ

    def body(one_ref, two_ref, out):
        total = one_ref[: 2 * NC] + two_ref[: 2 * NC]
        out[...] = jnp.broadcast_to(total[None], out.shape)

    return call(body, [like((peers, 2 * NC, one.shape[1]), one.dtype)], [one, two])


def finish(capped, stats, parents, prev_scores, penalty, after):
    rows, voc_rows = capped.shape
    steps = 4
    part = rows // steps

    def body(capped_ref, stats_ref, par_ref, prev_ref, pen_ref, after_ref, log_ref, chosen_ref, norm_ref, column):
        step = pl.program_id(0)

        @pl.when(step == 0)
        def _():
            sums = jnp.sum(stats_ref[...], axis=0)
            lse = jnp.log(sums)
            sub = lax.broadcasted_iota(jnp.int32, (LANES, LANES), 0)
            lane = lax.broadcasted_iota(jnp.int32, (1, LANES), 1)
            for h in range(rows // LANES):
                at = slice(h * LANES, (h + 1) * LANES)

                def down(row):
                    return jnp.broadcast_to(row, (LANES, LANES)).T

                lse_col = down(lse[h : h + 1])
                column[at] = lse_col
                hit = sub == lane // BEAMS * BEAMS + par_ref[:, at]
                lse_par = jnp.sum(jnp.where(hit, lse_col, 0.0), axis=0, keepdims=True)
                prev_par = jnp.sum(jnp.where(hit, down(prev_ref[:, at]), 0.0), axis=0, keepdims=True)
                chosen = sums[NC + h : NC + h + 1] - lse_par
                chosen_ref[:, at] = chosen
                norm_ref[:, at] = (prev_par + chosen) / pen_ref[:, at]

        lse_here = column[pl.ds(pl.multiple_of(step * part, part), part)]
        for start in range(0, voc_rows, LANES):
            at = slice(start, start + LANES)
            log_ref[:, at] = capped_ref[:, at] - lse_here

    block = pl.BlockSpec((part, voc_rows), lambda i: (i, 0))
    row = pl.BlockSpec((1, rows), lambda i: (0, 0))
    return pl.pallas_call(
        body,
        out_shape=[
            like((rows, voc_rows), jnp.float32), like((1, rows), jnp.float32), like((1, rows), jnp.float32)
        ],
        grid=(steps,),
        in_specs=[
            block, pl.BlockSpec(stats.shape, lambda i: (0, 0, 0)), row, row, row,
            pl.BlockSpec(memory_space=pl.ANY),
        ],
        out_specs=[block, row, row],
        scratch_shapes=[pltpu.VMEM((rows, LANES), jnp.float32)],
        cost_estimate=pl.CostEstimate(flops=0, bytes_accessed=0, transcendentals=0),
        compiler_params=pltpu.CompilerParams(vmem_limit_bytes=VMEM),
    )(capped, stats, parents, prev_scores, penalty, after)


def add(one, halves, after):
    count, depth = one.shape
    cuts = [slice(start, start + LANES) for start in range(0, count, LANES)]

    def body(one_ref, low_ref, high_ref, out, held, total, sems):
        load = []
        for n, at in enumerate(cuts):
            ref, start = (low_ref, at.start) if at.start < count // 2 else (high_ref, at.start - count // 2)
            load.append(
                [
                    pltpu.make_async_copy(one_ref.at[at], held.at[0, at], sems.at[0, n]),
                    pltpu.make_async_copy(ref.at[start : start + LANES], held.at[1, at], sems.at[1, n]),
                ]
            )
        put = [pltpu.make_async_copy(total.at[at], out.at[at], sems.at[2, n]) for n, at in enumerate(cuts)]
        for pair in load:
            start_all(pair)
        for n, at in enumerate(cuts):
            for copy in load[n]:
                copy.wait()
            total[at] = held[0, at] + held[1, at]
            put[n].start()
        for copy in put:
            copy.wait()

    return call(
        body, [pltpu.HBM(one.shape, one.dtype)], [one, *halves], after, far_args=1, any_args=2,
        scratch=[
            pltpu.VMEM((2, *one.shape), one.dtype),
            pltpu.VMEM(one.shape, one.dtype),
            pltpu.SemaphoreType.DMA((3, len(cuts))),
        ],
    )


def sum_rows(stacked, copies, after=()):
    terms, rows, depth = stacked.shape

    def body(in_ref, out):
        found = in_ref[0].astype(jnp.float32)
        for n in range(1, terms):
            found = found + in_ref[n].astype(jnp.float32)
        for n in range(copies):
            out[n] = found.astype(stacked.dtype)

    return call(body, [like((copies, rows, depth))], [stacked], after)


def assemble(place, mine, other):
    parts = len(mine)
    quarters, part, depth = mine[0].shape

    def body(place_ref, *refs):
        *pieces, out, sems = refs
        copies = []
        for n, ref in enumerate(pieces):
            core = place_ref[0] if n < parts else 1 - place_ref[0]
            x = lax.rem(place_ref[2] + parts - n % parts, parts)
            at = pl.ds(pl.multiple_of((core * parts + x) * part, part), part)
            for q in range(quarters):
                copies.append(
                    pltpu.make_async_copy(
                        ref.at[q], out.at[at, q * depth : (q + 1) * depth], sems.at[n, q]
                    )
                )
        start_all(copies)
        for copy in copies:
            copy.wait()

    return call(
        body, [pltpu.HBM((NC * parts * part, quarters * depth), mine[0].dtype)],
        [place, *mine, *other], smem=1,
        scratch=[pltpu.SemaphoreType.DMA((NC * parts, quarters))],
    )


def local(hidden, norm_gain, embed_table, tokens, parents, prev_scores, lengths):
    shard = lax.axis_index(VOC)
    core = lax.axis_index("c")
    y = lax.axis_index("y")
    voc_rows, depth = embed_table.shape
    row_count, width = hidden.shape
    scale = math.sqrt(width)
    place = jnp.stack([core, y, lax.axis_index("x")]).astype(jnp.int32)
    gain = norm_gain.reshape(1, width)
    part = row_count // (NC * NX)

    arrived = [tokens] + [shift(tokens, "y", NY, step) for step in (1, 2, 3)]
    pieces, t_cut = cut_pieces(place, hidden, gain, arrived[1:])
    arrived = jnp.stack(arrived)
    mine = exchange(pieces, "y")
    *others, _ = take_planes(place, mine, ((2, 3), (0, 1)))
    others = [shift(array, "c", NC, 1) for array in others]
    order = (y - jnp.arange(NY)) % NY
    planes = sum(jnp.where((order == s)[:, None], arrived[s : s + 1], 0) for s in range(NY))
    planes = (planes - shard * voc_rows).reshape(NY, NC, NX, part).transpose(1, 2, 0, 3)
    planes = jnp.where(core == 0, planes, planes[::-1]).reshape(NC * NX * NY * part, 1)

    *sent, kept, t_pick = pick_rows(planes, embed_table, scale, [t_cut])
    got = [shift(piece, "c", NC, 1) for piece in sent]
    row_scale, t_scale = scales(hidden, [t_pick])
    found, t_found = add(kept, got, [t_scale])
    found = exchange(found.reshape(NX * NY, part, depth), ("x", "y"))
    far_a, far_b, t_far = products(place, embed_table, mine, others[:1], (2,), (2,), [t_found])
    far_a = shift(far_a, "y", NY, 1)
    far_b = shift(far_b, "y", NY, 3)
    ahead, behind, t_all = products(place, embed_table, mine, others, (1, 3), (1, 1), [t_far])
    found, t_sum = sum_rows(found.reshape(NX, NY * part, depth), 1, [t_all])
    left, right, t_near = add_halves(ahead, behind, far_a, far_b, [t_sum])
    left = shift(left, "y", NY, 1)
    right = shift(right, "y", NY, 3)

    found = exchange(found.reshape(NZ, NY * part // NZ, depth), "z")
    own, t_own = products(place, embed_table, mine, others, (0,), (1,), [t_near])
    spread, t_z = sum_rows(found, NZ, [t_own])
    spread = exchange(spread, "z").reshape(NY, part, depth)

    local_col = tokens - shard * voc_rows
    capped, stats, t_cap = cap_and_sum(
        place, own, left, right, row_scale, local_col[None], parents[None], [spread]
    )
    stats, _ = spread_sum(stats, shift(stats, "c", NC, 1))
    stats = exchange(stats, ("x", "z"))
    penalty = jnp.power((5.0 + lengths.astype(jnp.float32)) / 6.0, length_power)
    parts = [spread] + [shift(spread, "x", NX, step) for step in (1, 2, 3)]
    next_embed, t_whole = assemble(place, parts, [shift(piece, "c", NC, 1) for piece in parts])
    log_probs, chosen_lp, normalized = finish(
        capped, stats, parents[None], prev_scores[None], penalty[None], t_whole
    )
    return (log_probs, chosen_lp[0], normalized[0], next_embed)


def solution(mesh):
    split = Mesh(mesh.devices.reshape(NX, NZ, NC, NY), VOC + ("y",))
    placed = (P("y", None), P(), P(VOC, "y"), P("y"), P("y"), P("y"), P("y"))
    return jax.shard_map(
        local,
        mesh=split,
        in_specs=placed,
        out_specs=(P("y", VOC), P("y"), P("y"), P("y", None)),
        check_vma=False,
    )
```
